32 devices in a mesh: graph: 2 (over core), dom: 16 (over z, y, x).
Axes of the slice: x: 2, y: 2, z: 4, core: 2. Of those that a mesh axis runs over, the one named last changes fastest.
Arguments:
- embeddings: float32 [2, 8192, 300], P('graph', 'dom'), may hold values from -6 to 6
- first_weight: float32 [300, 300], replicated, may hold values from -0.375 to 0.375
- second_weight: float32 [300, 300], replicated, may hold values from -0.375 to 0.375
- bound_index: int32 [2, 16, 2, 64], P('graph', 'dom'), may hold values from 0 to 511
- neighbors: int32 [2, 8192, 16], P('graph', 'dom'), may hold values from 0 to 639
- degree: int32 [2, 8192], P('graph', 'dom'), may hold values from 1 to 16
- send_index: int32 [2, 16, 32, 32], P('graph', 'dom'), may hold values from 0 to 512, as said below
- recv_count: int32 [2, 16, 32], P('graph', 'dom'), may hold values from 8 to 32, as said below
- pair_index: int32 [2, 16, 2, 128], P('graph', 'dom'), may hold values from 0 to 1023, as said below
Outputs:
- grad_embeddings: float32 [2, 8192, 300], P('graph', 'dom')
- grad_first: float32 [300, 300], replicated
- grad_second: float32 [300, 300], replicated
- cluster_loss: float32 [2, 16], P('graph', 'dom')
The draws below stay inside these ranges and needn't reach their ends.
Inputs may be any that keep to these rules, and one draw needn't show every extreme that they name: `send_index`: for each sending partition and owner, filled slots come first and hold local rows, the empty ones hold 512; every local row is sent exactly once; in each aligned group of four owners one receives 32 rows from every partition. `recv_count`: equals the number of filled slots that send_index gives for this owner and that partition. `pair_index`: entries are s * 32 + c. Side 0 names each of the first 8 slots of every graph-0 partition once, side 1 each of the first 8 slots of every graph-1 partition once.
All inputs are finite; a program needn't handle non-finite values.
Results may differ from the reference program's by a relative error of at most 0.0003.
Values sent between devices are 32-bit elements; how exact they have to be, the bound alone decides.
A program may use at most 64 MiB of HBM per device.

```python
import math
import jax
import jax.numpy as jnp
from jax import lax

FEAT = 300
DEG = 16
ROWS_DEV = 512
NENT = 8192
AVG = 16
CAP = 32
NPAIR = 128
BND = 64
N_DOM = 16


def route_counts(key):
    device_count = 2 * N_DOM
    group_count = device_count // 4
    base = jax.random.fold_in(key, 7)
    hot_place = jax.random.randint(jax.random.fold_in(base, 1), (group_count,), 0, 4)
    first_load = jax.random.randint(jax.random.fold_in(base, 2), (device_count, group_count), AVG // 2, 3 * AVG // 4 + 1)
    second_load = jax.random.randint(jax.random.fold_in(base, 3), (device_count, group_count), AVG // 2, 3 * AVG // 4 + 1)
    third_load = 2 * AVG - first_load - second_load
    stacked = jnp.stack([first_load, second_load, third_load], axis=2)
    places = jnp.arange(4, dtype=jnp.int32)
    ranked = places[None, :] - (places[None, :] > hot_place[:, None]).astype(jnp.int32)
    ranked = jnp.clip(ranked, 0, 2)
    picked = jnp.take_along_axis(stacked, jnp.broadcast_to(ranked[None], (device_count, group_count, 4)), axis=2)
    counts = jnp.where(places[None, None, :] == hot_place[None, :, None], 2 * AVG, picked)
    return counts.reshape(device_count, device_count).astype(jnp.int32)


def take_rows_drawn(table, row_ids):
    return table[row_ids]


def draw_send_index(key, part):
    device_count = 2 * N_DOM
    counts = route_counts(key)
    starts = jnp.cumsum(counts, axis=1) - counts
    keys = jax.random.split(jax.random.fold_in(key, 11), device_count)
    orders = jax.vmap(lambda sub_key: jax.random.permutation(sub_key, ROWS_DEV))(keys).astype(jnp.int32)
    slot_ids = jnp.arange(CAP, dtype=jnp.int32)
    positions = jnp.minimum(starts[:, :, None] + slot_ids[None, None, :], ROWS_DEV - 1)
    chosen = jax.vmap(take_rows_drawn)(orders, positions)
    filled = slot_ids[None, None, :] < counts[:, :, None]
    result = jnp.where(filled, chosen, ROWS_DEV)
    return result.reshape(2, N_DOM, device_count, CAP).astype(jnp.int32)


def draw_recv_count(key, part):
    counts = route_counts(key)
    return counts.T.reshape(2, N_DOM, 2 * N_DOM).astype(jnp.int32)


def draw_pair_index(key, part):
    device_count = 2 * N_DOM
    half_avg = AVG // 2
    candidate = jnp.arange(NPAIR, dtype=jnp.int32)
    source_part = candidate // half_avg
    slot_part = candidate % half_avg
    flat_zero = source_part * CAP + slot_part
    flat_one = (source_part + N_DOM) * CAP + slot_part
    keys_zero = jax.random.split(jax.random.fold_in(key, 21), device_count)
    keys_one = jax.random.split(jax.random.fold_in(key, 22), device_count)
    order_zero = jax.vmap(lambda sub_key: jax.random.permutation(sub_key, NPAIR))(keys_zero).astype(jnp.int32)
    order_one = jax.vmap(lambda sub_key: jax.random.permutation(sub_key, NPAIR))(keys_one).astype(jnp.int32)
    side_zero = flat_zero[order_zero]
    side_one = flat_one[order_one]
    stacked = jnp.stack([side_zero, side_one], axis=1)
    return stacked.reshape(2, N_DOM, 2, NPAIR).astype(jnp.int32)


def with_ends(values, own_key, low, high):
    dims = values.shape
    spot = [jax.random.randint(jax.random.fold_in(own_key, axis), (), 0, dims[axis]) for axis in range(len(dims))]
    values = values.at[tuple(spot)].set(low)
    longest = dims.index(max(dims))
    spot[longest] = (spot[longest] + 1) % dims[longest]
    return values.at[tuple(spot)].set(high)


def block_levels(stream_key, extent, pieces, least, high):
    def one(position, blocks):
        steps = jax.random.uniform(jax.random.fold_in(jax.random.fold_in(stream_key, 6), position), (blocks,), jnp.float32, least / len(pieces), high / len(pieces))
        return jnp.repeat(jnp.exp(steps), extent[position] // blocks).reshape((-1,) + (1,) * (len(extent) - position - 1))

    loudness = one(*pieces[0])
    for cut in pieces[1:]:
        loudness = loudness * one(*cut)
    return loudness


def normal_values(own_key, dims, width, limit, cuts=(), kind=jnp.bfloat16):
    array = jax.random.normal(own_key, dims, jnp.float32) * width
    if len(cuts) > 0:
        array = block_levels(own_key, dims, cuts, -0.22, 0.18) * array
    return jnp.clip(array, min=-limit, max=limit).astype(kind)


def setup_inputs(seed: int = 0) -> dict:
    streams_of = jax.random.split(jax.random.key(seed), 10)
    embeddings = normal_values(streams_of[0], (2, NENT, FEAT), 1.0, 6.0, ((0, 2), (1, 16)), jnp.float32)
    first_weight = normal_values(streams_of[1], (FEAT, FEAT), FEAT ** -0.5, 0.375, (), jnp.float32)
    second_weight = normal_values(streams_of[2], (FEAT, FEAT), FEAT ** -0.5, 0.375, (), jnp.float32)
    bound_index = with_ends(jax.random.randint(streams_of[3], (2, N_DOM, 2, BND), 0, ROWS_DEV), jax.random.fold_in(streams_of[3], 1), 0, ROWS_DEV - 1).astype(jnp.int32)
    neighbors = with_ends(jax.random.randint(streams_of[4], (2, NENT, DEG), 0, ROWS_DEV + 2 * BND), jax.random.fold_in(streams_of[4], 1), 0, (ROWS_DEV + 2 * BND) - 1).astype(jnp.int32)
    degree = with_ends(jax.random.randint(streams_of[5], (2, NENT), 1, DEG + 1), jax.random.fold_in(streams_of[5], 1), 1, DEG).astype(jnp.int32)
    send_index = draw_send_index(jax.random.fold_in(streams_of[9], 71), 0)
    recv_count = draw_recv_count(jax.random.fold_in(streams_of[9], 71), 0)
    pair_index = draw_pair_index(jax.random.fold_in(streams_of[9], 71), 0)
    return {"embeddings": embeddings, "first_weight": first_weight, "second_weight": second_weight, "bound_index": bound_index, "neighbors": neighbors, "degree": degree, "send_index": send_index, "recv_count": recv_count, "pair_index": pair_index}


SOFTMAX_HEAT = 0.02
EPSILON = 1e-06
TOP_PRECISION = lax.Precision.HIGHEST

def aggregate(pool, neighbor_ids, degree_row):
    row_count = neighbor_ids.shape[0]
    rim_width = (pool.shape[0] - row_count) // 2
    running = pool[rim_width:rim_width + row_count]
    slot_ids = jnp.arange(neighbor_ids.shape[1], dtype=jnp.int32)
    live_mask = (slot_ids[None, :] < degree_row[:, None]).astype(jnp.float32)
    for offset_at in range(0, neighbor_ids.shape[1], 4):
        picked = pool[neighbor_ids[:, offset_at:offset_at + 4]]
        running = running + lax.optimization_barrier(jnp.sum(picked * live_mask[:, offset_at:offset_at + 4, None], axis=1))
    return running / (1.0 + degree_row.astype(jnp.float32))[:, None]

def cluster_term(incoming_rows, counts, pair_rows):
    slot_total = incoming_rows.shape[0]
    slot_cap = slot_total // counts.shape[0]
    live_mask = (jnp.arange(slot_cap, dtype=jnp.int32)[None, :] < counts[:, None]).reshape(slot_total)
    half_slot_count = slot_total // 2
    source_entity = incoming_rows[pair_rows[0]]
    target_entity = incoming_rows[pair_rows[1]]
    first_layer_logits = jnp.dot(source_entity, incoming_rows[half_slot_count:].T, precision=TOP_PRECISION, preferred_element_type=jnp.float32) / SOFTMAX_HEAT
    second_layer_logits = jnp.dot(target_entity, incoming_rows[:half_slot_count].T, precision=TOP_PRECISION, preferred_element_type=jnp.float32) / SOFTMAX_HEAT
    first_total = jnp.log(lax.optimization_barrier(jnp.sum(jnp.where(live_mask[half_slot_count:][None, :], jnp.exp(first_layer_logits), 0.0), axis=1)))
    second_total = jnp.log(lax.optimization_barrier(jnp.sum(jnp.where(live_mask[:half_slot_count][None, :], jnp.exp(second_layer_logits), 0.0), axis=1)))
    positive_match = lax.optimization_barrier(jnp.sum(source_entity * target_entity, axis=1)) / SOFTMAX_HEAT
    return jnp.sum(first_total + second_total - 2.0 * positive_match)

def take_rows(table, row_ids):
    return table[row_ids]

def reference(embeddings, first_weight, second_weight, bound_index, neighbors, degree, send_index, recv_count, pair_index):
    feat_width = embeddings.shape[2]
    device_count = 2 * N_DOM
    neighbor_all = neighbors.reshape(device_count, ROWS_DEV, DEG)
    degree_all = degree.reshape(device_count, ROWS_DEV)
    routes = send_index.reshape(device_count, device_count, CAP)

    def fetch(table):
        lower_part = jax.vmap(jax.vmap(take_rows))(table, bound_index[:, :, 0])
        upper_part = jax.vmap(jax.vmap(take_rows))(table, bound_index[:, :, 1])
        from_below = jnp.roll(upper_part, 1, axis=1)
        from_above = jnp.roll(lower_part, -1, axis=1)
        return jnp.concatenate([from_below, table, from_above], axis=2)

    def layer(table, weight):
        pool = fetch(table).reshape(device_count, ROWS_DEV + 2 * BND, feat_width)

        def per_device(packed):
            pool_rows, neighbor_ids, degree_row = packed
            return jnp.dot(aggregate(pool_rows, neighbor_ids, degree_row), weight, precision=TOP_PRECISION, preferred_element_type=jnp.float32)
        outputs = lax.map(per_device, (pool, neighbor_all, degree_all))
        return outputs.reshape(2, N_DOM, ROWS_DEV, feat_width)

    def objective(emb_table, weight_one, weight_two):
        inputs = emb_table.reshape(2, N_DOM, ROWS_DEV, feat_width)
        hidden = jnp.tanh(layer(inputs, weight_one))
        latent = layer(hidden, weight_two)
        unit_rows = latent / jnp.sqrt(lax.optimization_barrier(jnp.sum(latent * latent, axis=-1, keepdims=True)) + EPSILON)
        padded = jnp.concatenate([unit_rows.reshape(device_count, ROWS_DEV, feat_width), jnp.zeros((device_count, 1, feat_width), jnp.float32)], axis=1)

        def cluster(packed):
            owner, counts, pair_rows = packed
            slot_rows = jnp.take(routes, owner, axis=1)
            incoming_rows = jax.vmap(take_rows)(padded, slot_rows).reshape(device_count * CAP, feat_width)
            return cluster_term(incoming_rows, counts, pair_rows)
        losses = lax.map(cluster, (jnp.arange(device_count, dtype=jnp.int32), recv_count.reshape(device_count, device_count), pair_index.reshape(device_count, 2, NPAIR)))
        return (jnp.sum(losses), losses)
    (total, losses), grads = jax.value_and_grad(objective, argnums=(0, 1, 2), has_aux=True)(embeddings, first_weight, second_weight)
    grad_scale = 1.0 / math.sqrt(2 * NENT)
    return (grads[0], grads[1] * grad_scale, grads[2] * grad_scale, (losses / (2.0 * NPAIR)).reshape(2, N_DOM))
```

```python
import functools
import math

import jax
import jax.numpy as jnp
from jax import lax
from jax.experimental import pallas as pl
from jax.experimental.pallas import tpu as pltpu
from jax.sharding import PartitionSpec as P

HEAT = 1.0 / 0.02
EPSILON = 1e-06
F32 = jnp.float32
BF16 = jnp.bfloat16
MESH = pl.DeviceIdType.MESH


def pieces(x):
    high = x.astype(BF16)
    return high, (x - high.astype(F32)).astype(BF16)


def mm(a, b, ca=1, cb=0):
    return lax.dot_general(a, b, (((ca,), (cb,)), ((), ())), preferred_element_type=F32)


def mm2(exact, x, ca=1, cb=0):
    high, low = pieces(x)
    return mm(exact, high, ca, cb) + mm(exact, low, ca, cb)


def mm3(a, b, ca=1, cb=0):
    ah, al = pieces(a)
    bh, bl = pieces(b)
    return mm(ah, bh, ca, cb) + (mm(ah, bl, ca, cb) + mm(al, bh, ca, cb))


def one_hot(ids, shape, axis):
    return (ids == lax.broadcasted_iota(jnp.int32, shape, axis)).astype(F32).astype(BF16)


def kernel(
    sizes,
    emb_ref,
    w1_ref,
    w2_ref,
    nb_ref,
    cols_ref,
    rows_ref,
    gemb_ref,
    g1_ref,
    g2_ref,
    loss_ref,
    x_s,
    w1_s,
    w2_s,
    adj,
    mix1,
    mix2,
    hid,
    unit_s,
    out1,
    in1,
    out2,
    in2,
    rec,
    hs,
    hr,
    pk,
    pair_in,
    half_s,
    rs_in,
    red,
    fin,
    halo_ss,
    halo_rs,
    a_ss,
    a_rs,
    pair_ss,
    pair_rs,
    rs_ss,
    rs_rs,
    ag_ss,
    ag_rs,
    back_ss,
    back_rs,
):
    n_graph, n_dom, cap, feat, rows, rim, n_pair = sizes
    n_dev = n_graph * n_dom
    slots = n_dev * cap
    half = slots // 2
    wide = x_s.shape[1]
    part = in1.shape[1] - 2 * cap
    packed = part != cap
    my_g = lax.axis_index("graph")
    my_d = lax.axis_index("dom")
    me = my_g * n_dom + my_d
    other = 1 - my_g
    below = lax.rem(my_d + n_dom - 1, n_dom)
    above = lax.rem(my_d + 1, n_dom)

    barrier = pltpu.get_barrier_semaphore()

    def greet(k, carry):
        o = lax.rem(me + k, n_dev)
        pl.semaphore_signal(
            barrier, inc=1, device_id=(o // n_dom, lax.rem(o, n_dom)), device_id_type=MESH
        )
        return carry

    lax.fori_loop(1, n_dev, greet, 0)

    def remote(src, dst, ss, rs, device):
        return pltpu.make_async_remote_copy(
            src_ref=src, dst_ref=dst, send_sem=ss, recv_sem=rs, device_id=device, device_id_type=MESH
        )

    def halo(p):
        return (
            remote(hs.at[p, 0], hr.at[p, 1], halo_ss.at[p, 0], halo_rs.at[p, 1], (my_g, below)),
            remote(hs.at[p, 1], hr.at[p, 0], halo_ss.at[p, 1], halo_rs.at[p, 0], (my_g, above)),
        )

    def send_halo(p, edge):
        hs[p] = edge.reshape(2, rim, wide)
        for copy in halo(p):
            copy.start()

    def take_halo(p):
        for copy in halo(p):
            copy.wait()
        return hr[p].reshape(2 * rim, wide)

    x_s[...] = jnp.zeros_like(x_s)
    x_s[:, 0:feat] = emb_ref[...]
    x = x_s[...]
    bsel = one_hot(cols_ref[0 : 2 * rim, 1:2], (2 * rim, rows), 1)
    edge = mm2(bsel, x)
    pl.semaphore_wait(barrier, n_dev - 1)
    send_halo(0, edge)

    for dst, src in ((w1_s, w1_ref), (w2_s, w2_ref)):
        dst[...] = jnp.zeros_like(dst)
        dst[0:feat, 0:feat] = src[...]

    block = 32

    def build(i, carry):
        at = pl.multiple_of(i * block, block)
        c = lax.broadcasted_iota(jnp.int32, (block, rows + 2 * rim), 1)
        r = lax.broadcasted_iota(jnp.int32, (block, rows + 2 * rim), 0) + at
        ids = jnp.where(c < rows, c + rim, jnp.where(c < rows + rim, c - rows, c))
        nb = nb_ref[pl.ds(at, block), :]
        deg = cols_ref[pl.ds(at, block), 3:4]
        k = lax.broadcasted_iota(jnp.int32, nb.shape, 1)
        nb = jnp.where(k < deg, nb, -1)
        total = jnp.where(c == r, 1.0, 0.0)
        for j in range(nb.shape[1]):
            total = total + jnp.where(nb[:, j : j + 1] == ids, 1.0, 0.0)
        adj[pl.ds(at, block), :] = total.astype(BF16)
        return carry

    lax.fori_loop(0, rows // block, build, 0)
    inv = 1.0 / (1.0 + cols_ref[0:rows, 3:4].astype(F32))

    own = mm2(adj[:, 0:rows], x)
    mix1[...] = (own + mm2(adj[:, rows:], take_halo(0))) * inv
    hid[...] = jnp.tanh(mm3(mix1[...], w1_s[...]))
    hidden = hid[...]
    send_halo(1, mm2(bsel, hidden))
    own = mm2(adj[:, 0:rows], hidden)
    mix2[...] = (own + mm2(adj[:, rows:], take_halo(1))) * inv
    latent = mm3(mix2[...], w2_s[...])
    inv_len = 1.0 / jnp.sqrt(jnp.sum(latent * latent, axis=1, keepdims=True) + EPSILON)
    unit_s[...] = latent * inv_len

    def put(ref, m, first):
        count = m.shape[0] // cap
        ref[first : first + count, 0:cap, :] = m[:, 0:128].reshape(count, cap, 128)
        ref[first : first + count, cap : 2 * cap, :] = m[:, 128:256].reshape(count, cap, 128)
        last = m[:, 256:384].reshape(count, cap, 128)
        if packed:
            late = pltpu.roll(last[:, part:].reshape(count * part, 128), 64, 1)
            last = last[:, 0:part] + late.reshape(count, part, 128)
        ref[first : first + count, 2 * cap :, :] = last

    def get(ref, dst):
        dst[:, 0:128] = ref[:, 0:cap, :].reshape(slots, 128)
        dst[:, 128:256] = ref[:, cap : 2 * cap, :].reshape(slots, 128)
        last = ref[:, 2 * cap :, :]
        if packed:
            flat = last.reshape(n_dev * part, 128)
            keep = lax.broadcasted_iota(jnp.int32, flat.shape, 1) < 64
            early = jnp.where(keep, flat, 0.0).reshape(n_dev, part, 128)
            late = jnp.where(keep, pltpu.roll(flat, 64, 1), 0.0).reshape(n_dev, part, 128)
            last = jnp.concatenate([early, late], axis=1)
        dst[:, 256:384] = last.reshape(slots, 128)

    def to_owner(q, src, dst, o, land):
        return remote(
            src.at[o],
            dst.at[land],
            a_ss.at[q, o],
            a_rs.at[q, land],
            (o // n_dom, lax.rem(o, n_dom)),
        )

    def send_part(q, src, dst, graph):
        def step(k, carry):
            d = lax.rem(my_d + k, n_dom)
            o = graph * n_dom + d

            @pl.when(o != me)
            def _():
                to_owner(q, src, dst, o, me).start()

            return carry

        lax.fori_loop(0, n_dom, step, 0)

    def wait_all(q, src, dst):
        def step(k, carry):
            o = lax.rem(me + k, n_dev)
            to_owner(q, src, dst, o, o).wait()
            return carry

        lax.fori_loop(1, n_dev, step, 0)
        dst[pl.ds(me, 1)] = src[pl.ds(me, 1)]

    for graph in range(n_graph):
        lo = graph * half
        route = one_hot(cols_ref[lo : lo + half, 0:1], (half, rows), 1)
        put(out1, mm2(route, unit_s[...]), graph * n_dom)
        send_part(0, out1, in1, graph)

    unroute = one_hot(rows_ref[0:1, :], (rows, slots), 0)
    unbound = one_hot(rows_ref[1:2, 0 : 2 * rim], (rows, 2 * rim), 0)
    pair_a = one_hot(cols_ref[0:n_pair, 2:3], (n_pair, half), 1)
    pair_b = one_hot(cols_ref[n_pair : 2 * n_pair, 2:3] - half, (n_pair, half), 1)
    live = rows_ref[2:3, :].astype(F32)

    wait_all(0, out1, in1)
    get(in1, rec)
    r0 = rec[0:half]
    r1 = rec[half:slots]
    a = mm2(pair_a, r0)
    b = mm2(pair_b, r1)
    e1 = jnp.exp(mm3(a, r1, 1, 1) * HEAT) * live[:, half:]
    e2 = jnp.exp(mm3(b, r0, 1, 1) * HEAT) * live[:, :half]
    t1 = jnp.sum(e1, axis=1, keepdims=True)
    t2 = jnp.sum(e2, axis=1, keepdims=True)
    s1 = e1 * (1.0 / t1)
    s2 = e2 * (1.0 / t2)
    match = jnp.sum(a * b, axis=1, keepdims=True) * HEAT
    loss_ref[...] = jnp.sum(jnp.log(t1) + jnp.log(t2) - 2.0 * match, axis=0, keepdims=True) * (
        1.0 / (2.0 * n_pair)
    )
    da = HEAT * (mm3(s1, r1) - 2.0 * b)
    put(out2, mm3(s2, HEAT * b, 0, 0) + mm2(pair_a, da, 0, 0), 0)
    send_part(1, out2, in2, 0)
    db = HEAT * (mm3(s2, r0) - 2.0 * a)
    put(out2, mm3(s1, HEAT * a, 0, 0) + mm2(pair_b, db, 0, 0), n_dom)
    send_part(1, out2, in2, 1)
    wait_all(1, out2, in2)
    get(in2, rec)

    tall = -(-feat // 16) * 16
    chunk = half_s.shape[2]

    def pack_sum(w, g):
        last = g[0:tall, 256:384]
        last = last[0 : tall // 2] + pltpu.roll(last[tall // 2 :], 64, 1)
        spare = jnp.zeros((n_dev * chunk - 5 * tall // 2, 128), F32)
        flat = jnp.concatenate([g[0:tall, 0:128], g[0:tall, 128:256], last, spare], axis=0)
        pk[w] = flat.reshape(n_graph, n_dom, chunk, 128)

    def pair_copy(w):
        return remote(
            pk.at[w, other], pair_in.at[w], pair_ss.at[w], pair_rs.at[w], (other, my_d)
        )

    def scatter_copy(w, d, land):
        return remote(
            half_s.at[w, d], rs_in.at[w, land], rs_ss.at[w, d], rs_rs.at[w, land], (my_g, d)
        )

    def gather_copy(w, d, land):
        return remote(
            red.at[w], fin.at[w, my_g, land], ag_ss.at[w, d], ag_rs.at[w, land], (my_g, d)
        )

    def each_chip(do):
        def step(k, carry):
            do(lax.rem(my_d + k, n_dom))
            return carry

        lax.fori_loop(1, n_dom, step, 0)

    def sum_scatter(w):
        pair_copy(w).wait()
        half_s[w] = pk[w, pl.ds(my_g, 1)].reshape(n_dom, chunk, 128) + pair_in[w]
        each_chip(lambda d: scatter_copy(w, d, my_d).start())

    def sum_gather(w):
        each_chip(lambda d: scatter_copy(w, d, d).wait())
        rs_in[w, pl.ds(my_d, 1)] = half_s[w, pl.ds(my_d, 1)]
        total = jnp.sum(rs_in[w], axis=0) * (1.0 / math.sqrt(rows * n_dev))
        red[w] = total
        fin[w, pl.ds(my_g, 1), pl.ds(my_d, 1)] = total.reshape(1, 1, chunk, 128)
        each_chip(lambda d: gather_copy(w, d, my_d).start())

    def back_copy(w, side):
        return remote(
            fin.at[w, my_g], fin.at[w, side], back_ss.at[w], back_rs.at[w], (other, my_d)
        )

    def sum_back(w):
        each_chip(lambda d: gather_copy(w, d, d).wait())
        back_copy(w, my_g).start()

    def sum_end(w, ref):
        back_copy(w, my_g).wait_send()
        back_copy(w, other).wait_recv()
        flat = fin[w].reshape(n_dev * chunk, 128)
        ref[:, 0:128] = flat[0:feat]
        ref[:, 128:256] = flat[tall : tall + feat]
        last = flat[2 * tall : 2 * tall + tall // 2]
        last = jnp.concatenate([last, pltpu.roll(last, 64, 1)], axis=0)
        ref[:, 256:feat] = last[0:feat, 0 : feat - 256]

    unit = unit_s[...]
    grad_unit = mm2(unroute, rec[...])
    grad_latent = (
        grad_unit - unit * jnp.sum(grad_unit * unit, axis=1, keepdims=True)
    ) * inv_len
    pack_sum(1, mm3(mix2[...], grad_latent, 0, 0))
    pair_copy(1).start()
    grad_mix = mm3(grad_latent, w2_s[...], 1, 1) * inv
    send_halo(2, mm2(adj[:, rows:], grad_mix, 0, 0))
    own = mm2(adj[:, 0:rows], grad_mix, 0, 0)
    sum_scatter(1)
    grad_hidden = own + mm2(unbound, take_halo(2))
    hidden = hid[...]
    grad_inner = grad_hidden * (1.0 - hidden * hidden)
    pack_sum(0, mm3(mix1[...], grad_inner, 0, 0))
    pair_copy(0).start()
    grad_mix = mm3(grad_inner, w1_s[...], 1, 1) * inv
    sum_scatter(0)
    sum_gather(1)
    send_halo(3, mm2(adj[:, rows:], grad_mix, 0, 0))
    own = mm2(adj[:, 0:rows], grad_mix, 0, 0)
    sum_gather(0)
    sum_back(1)
    grad_x = own + mm2(unbound, take_halo(3))
    gemb_ref[...] = grad_x[:, 0:feat]
    sum_end(1, g2_ref)
    sum_back(0)
    sum_end(0, g1_ref)


def on_device(
    embeddings,
    first_weight,
    second_weight,
    bound_index,
    neighbors,
    degree,
    send_index,
    recv_count,
    pair_index,
):
    rows, feat = embeddings.shape[1:]
    rim = bound_index.shape[-1]
    n_graph = lax.axis_size("graph")
    n_dom = lax.axis_size("dom")
    n_dev = n_graph * n_dom
    cap = send_index.shape[-1]
    n_pair = pair_index.shape[-1]
    slots = n_dev * cap
    wide = -(-feat // 128) * 128
    pool = rows + 2 * rim

    live = jnp.arange(cap, dtype=jnp.int32)[None, :] < recv_count[0, 0][:, None]

    def line(v):
        v = v.reshape(-1)
        return jnp.pad(v, (0, slots - v.shape[0]))

    table = jnp.stack(
        [
            line(send_index),
            line(bound_index),
            line(pair_index),
            line(degree),
        ]
    )
    rows_in = jnp.stack(
        [
            line(send_index),
            line(bound_index),
            line(live.astype(jnp.int32)),
        ]
    )

    part = cap // 2 if cap % 16 == 0 else cap
    tall = -(-feat // 16) * 16
    chunk = -(-(5 * tall // 2) // (8 * n_dev)) * 8
    sem = pltpu.SemaphoreType.DMA
    vmem = pltpu.VMEM
    sizes = (n_graph, n_dom, cap, feat, rows, rim, n_pair)
    grad_emb, g1, g2, loss = pl.pallas_call(
        functools.partial(kernel, sizes),
        out_shape=(
            jax.ShapeDtypeStruct((rows, feat), F32),
            jax.ShapeDtypeStruct((feat, feat), F32),
            jax.ShapeDtypeStruct((feat, feat), F32),
            jax.ShapeDtypeStruct((1, 1), F32),
        ),
        in_specs=[pl.BlockSpec(memory_space=pltpu.VMEM)] * 6,
        out_specs=[pl.BlockSpec(memory_space=pltpu.VMEM)] * 4,
        scratch_shapes=[
            vmem((rows, wide), F32),
            vmem((wide, wide), F32),
            vmem((wide, wide), F32),
            vmem((rows, pool), BF16),
            vmem((rows, wide), F32),
            vmem((rows, wide), F32),
            vmem((rows, wide), F32),
            vmem((rows, wide), F32),
            vmem((n_dev, 2 * cap + part, 128), F32),
            vmem((n_dev, 2 * cap + part, 128), F32),
            vmem((n_dev, 2 * cap + part, 128), F32),
            vmem((n_dev, 2 * cap + part, 128), F32),
            vmem((slots, wide), F32),
            vmem((4, 2, rim, wide), F32),
            vmem((4, 2, rim, wide), F32),
            vmem((2, n_graph, n_dom, chunk, 128), F32),
            vmem((2, n_dom, chunk, 128), F32),
            vmem((2, n_dom, chunk, 128), F32),
            vmem((2, n_dom, chunk, 128), F32),
            vmem((2, chunk, 128), F32),
            vmem((2, n_graph, n_dom, chunk, 128), F32),
            sem((4, 2)),
            sem((4, 2)),
            sem((2, n_dev)),
            sem((2, n_dev)),
            sem((2,)),
            sem((2,)),
            sem((2, n_dom)),
            sem((2, n_dom)),
            sem((2, n_dom)),
            sem((2, n_dom)),
            sem((2,)),
            sem((2,)),
        ],
        compiler_params=pltpu.CompilerParams(
            collective_id=0, has_side_effects=True, vmem_limit_bytes=50 * 1024 * 1024
        ),
    )(embeddings[0], first_weight, second_weight, neighbors[0], table.T, rows_in)
    return grad_emb[None], g1, g2, loss


def solution(mesh):
    in_specs = (
        P("graph", "dom", None),
        P(),
        P(),
        P("graph", "dom", None, None),
        P("graph", "dom", None),
        P("graph", "dom"),
        P("graph", "dom", None, None),
        P("graph", "dom", None),
        P("graph", "dom", None, None),
    )
    out_specs = (P("graph", "dom", None), P(), P(), P("graph", "dom"))
    return jax.shard_map(
        on_device, mesh=mesh, in_specs=in_specs, out_specs=out_specs, check_vma=False
    )
```

```python
import functools
import math

import jax
import jax.numpy as jnp
from jax import lax
from jax.experimental import pallas as pl
from jax.experimental.pallas import tpu as pltpu
from jax.sharding import PartitionSpec as P

HEAT = 1.0 / 0.02
EPSILON = 1e-06
F32 = jnp.float32
BF16 = jnp.bfloat16
MESH = pl.DeviceIdType.MESH


def pieces(x):
    high = x.astype(BF16)
    return high, (x - high.astype(F32)).astype(BF16)


def mm(a, b, ca=1, cb=0):
    return lax.dot_general(a, b, (((ca,), (cb,)), ((), ())), preferred_element_type=F32)


def both(x, axis=1):
    return jnp.concatenate(pieces(x), axis=axis)


def mm2(exact, x, ca=1, cb=0):
    width = x.shape[1 - cb]
    full = mm(exact, both(x, 1 - cb), ca, cb)
    return full[:, 0:width] + full[:, width:]


def mm3(a, b, ca=1, cb=0):
    ah, al = pieces(a)
    bh, bl = pieces(b)
    width = b.shape[1 - cb]
    full = mm(ah, jnp.concatenate([bh, bl], axis=1 - cb), ca, cb)
    return full[:, 0:width] + (full[:, width:] + mm(al, bh, ca, cb))


def one_hot(ids, shape, axis):
    return (ids == lax.broadcasted_iota(jnp.int32, shape, axis)).astype(F32).astype(BF16)


def kernel(
    sizes,
    emb_ref,
    w1_ref,
    w2_ref,
    nb_ref,
    deg_ref,
    send_ref,
    bound_ref,
    count_ref,
    pairs_ref,
    gemb_ref,
    g1_ref,
    g2_ref,
    loss_ref,
    x_s,
    w1_s,
    w2_s,
    ids_s,
    cols_s,
    adj,
    adj_t,
    mix1,
    mix2,
    hid,
    unit_s,
    out1,
    in1,
    out2,
    in2,
    rec,
    hs,
    hr,
    pk,
    pair_in,
    half_s,
    rs_in,
    red,
    fin,
    halo_ss,
    halo_rs,
    a_ss,
    a_rs,
    pair_ss,
    pair_rs,
    rs_ss,
    rs_rs,
    ag_ss,
    ag_rs,
    back_ss,
    back_rs,
):
    n_graph, n_dom, cap, feat, rows, rim, n_pair = sizes
    n_dev = n_graph * n_dom
    slots = n_dev * cap
    half = slots // 2
    wide = x_s.shape[1]
    part = in1.shape[1] - 2 * cap
    packed = part != cap
    my_g = lax.axis_index("graph")
    my_d = lax.axis_index("dom")
    me = my_g * n_dom + my_d
    other = 1 - my_g
    below = lax.rem(my_d + n_dom - 1, n_dom)
    above = lax.rem(my_d + 1, n_dom)

    barrier = pltpu.get_barrier_semaphore()

    def greet(k, carry):
        o = lax.rem(me + k, n_dev)
        pl.semaphore_signal(
            barrier, inc=1, device_id=(o // n_dom, lax.rem(o, n_dom)), device_id_type=MESH
        )
        return carry

    lax.fori_loop(1, n_dev, greet, 0)

    def remote(src, dst, ss, rs, device):
        return pltpu.make_async_remote_copy(
            src_ref=src, dst_ref=dst, send_sem=ss, recv_sem=rs, device_id=device, device_id_type=MESH
        )

    def halo(p):
        return (
            remote(hs.at[p, 0], hr.at[p, 1], halo_ss.at[p, 0], halo_rs.at[p, 1], (my_g, below)),
            remote(hs.at[p, 1], hr.at[p, 0], halo_ss.at[p, 1], halo_rs.at[p, 0], (my_g, above)),
        )

    def send_halo(p, edge):
        hs[p] = edge.reshape(2, rim, wide)
        for copy in halo(p):
            copy.start()

    def take_halo(p):
        for copy in halo(p):
            copy.wait()
        return hr[p].reshape(2 * rim, wide)

    x_s[...] = jnp.zeros_like(x_s)
    x_s[:, 0:feat] = emb_ref[...]
    x = x_s[...]
    ids_s[...] = jnp.zeros_like(ids_s)
    ids_s[0:1, :] = send_ref[...]
    ids_s[1:2, 0 : 2 * rim] = bound_ref[...]
    ids_s[2:3, 0:n_pair] = pairs_ref[0:1, :]
    ids_s[2:3, n_pair : 2 * n_pair] = pairs_ref[1:2, :]
    ids_s[3:4, 0:rows] = deg_ref[...]
    cols_s[...] = jnp.transpose(ids_s[...].astype(F32)).astype(jnp.int32)
    bsel = one_hot(cols_s[0 : 2 * rim, 1:2], (2 * rim, rows), 1)
    edge = mm2(bsel, x)
    pl.semaphore_wait(barrier, n_dev - 1)
    send_halo(0, edge)

    for dst, src in ((w1_s, w1_ref), (w2_s, w2_ref)):
        dst[...] = jnp.zeros_like(dst)
        dst[0:feat, 0:feat] = src[...]

    block = 32
    slot = lax.broadcasted_iota(jnp.int32, nb_ref.shape, 0)
    near = jnp.where(slot < deg_ref[...], nb_ref[...], -1)

    def build(i, carry):
        at = pl.multiple_of(i * block, block)
        p = lax.broadcasted_iota(jnp.int32, (block, rows), 0) + at
        r = lax.broadcasted_iota(jnp.int32, (block, rows), 1)
        ids = jnp.where(p < rows, p + rim, jnp.where(p < rows + rim, p - rows, p))
        total = jnp.where(p == r, 1.0, 0.0)
        for j in range(near.shape[0]):
            total = total + jnp.where(near[j : j + 1, :] == ids, 1.0, 0.0)
        adj_t[pl.ds(at, block), :] = total.astype(BF16)
        return carry

    lax.fori_loop(0, (rows + 2 * rim) // block, build, 0)
    for at in range(0, rows + 2 * rim, 128):
        turned = jnp.transpose(adj_t[at : at + 128, :].astype(F32))
        adj[:, at : at + 128] = turned.astype(BF16)
    inv = 1.0 / (1.0 + cols_s[0:rows, 3:4].astype(F32))

    own = mm2(adj[:, 0:rows], x)
    mix1[...] = (own + mm2(adj[:, rows:], take_halo(0))) * inv
    send_halo(1, jnp.tanh(mm3(mm2(bsel, mix1[...]), w1_s[...])))
    hid[...] = jnp.tanh(mm3(mix1[...], w1_s[...]))
    own = mm2(adj[:, 0:rows], hid[...])
    mix2[...] = (own + mm2(adj[:, rows:], take_halo(1))) * inv
    latent = mm3(mix2[...], w2_s[...])
    inv_len = 1.0 / jnp.sqrt(jnp.sum(latent * latent, axis=1, keepdims=True) + EPSILON)
    unit_s[...] = latent * inv_len

    def put(ref, m, first):
        count = m.shape[0] // cap
        ref[first : first + count, 0:cap, :] = m[:, 0:128].reshape(count, cap, 128)
        ref[first : first + count, cap : 2 * cap, :] = m[:, 128:256].reshape(count, cap, 128)
        last = m[:, 256:384].reshape(count, cap, 128)
        if packed:
            late = pltpu.roll(last[:, part:].reshape(count * part, 128), 64, 1)
            last = last[:, 0:part] + late.reshape(count, part, 128)
        ref[first : first + count, 2 * cap :, :] = last

    def get(ref, dst):
        dst[:, 0:128] = ref[:, 0:cap, :].reshape(slots, 128)
        dst[:, 128:256] = ref[:, cap : 2 * cap, :].reshape(slots, 128)
        last = ref[:, 2 * cap :, :]
        if packed:
            flat = last.reshape(n_dev * part, 128)
            keep = lax.broadcasted_iota(jnp.int32, flat.shape, 1) < 64
            early = jnp.where(keep, flat, 0.0).reshape(n_dev, part, 128)
            late = jnp.where(keep, pltpu.roll(flat, 64, 1), 0.0).reshape(n_dev, part, 128)
            last = jnp.concatenate([early, late], axis=1)
        dst[:, 256:384] = last.reshape(slots, 128)

    def to_owner(q, src, dst, o, land):
        return remote(
            src.at[o],
            dst.at[land],
            a_ss.at[q, o],
            a_rs.at[q, land],
            (o // n_dom, lax.rem(o, n_dom)),
        )

    def send_part(q, src, dst, graph):
        def step(k, carry):
            d = lax.rem(my_d + k, n_dom)
            o = graph * n_dom + d

            @pl.when(o != me)
            def _():
                to_owner(q, src, dst, o, me).start()

            return carry

        lax.fori_loop(0, n_dom, step, 0)

    def wait_all(q, src, dst):
        def step(k, carry):
            o = lax.rem(me + k, n_dev)
            to_owner(q, src, dst, o, o).wait()
            return carry

        lax.fori_loop(1, n_dev, step, 0)
        dst[pl.ds(me, 1)] = src[pl.ds(me, 1)]

    for graph in range(n_graph):
        lo = graph * half
        route = one_hot(cols_s[lo : lo + half, 0:1], (half, rows), 1)
        put(out1, mm2(route, unit_s[...]), graph * n_dom)
        send_part(0, out1, in1, graph)

    unroute = one_hot(ids_s[0:1, :], (rows, slots), 0)
    unbound = one_hot(ids_s[1:2, 0 : 2 * rim], (rows, 2 * rim), 0)
    pair_a = one_hot(cols_s[0:n_pair, 2:3], (n_pair, half), 1)
    pair_b = one_hot(cols_s[n_pair : 2 * n_pair, 2:3] - half, (n_pair, half), 1)
    source = lax.broadcasted_iota(jnp.int32, (n_dev, slots), 0)
    place = lax.broadcasted_iota(jnp.int32, (n_dev, slots), 1) - source * cap
    inside = jnp.where((place >= 0) & (place < count_ref[...]), 1.0, 0.0)
    live = jnp.sum(inside, axis=0, keepdims=True)

    wait_all(0, out1, in1)
    get(in1, rec)
    r0 = rec[0:half]
    r1 = rec[half:slots]
    a = mm2(pair_a, r0)
    b = mm2(pair_b, r1)
    e1 = jnp.exp(mm3(a, r1, 1, 1) * HEAT) * live[:, half:]
    e2 = jnp.exp(mm3(b, r0, 1, 1) * HEAT) * live[:, :half]
    t1 = jnp.sum(e1, axis=1, keepdims=True)
    t2 = jnp.sum(e2, axis=1, keepdims=True)
    s1 = e1 * (1.0 / t1)
    s2 = e2 * (1.0 / t2)
    match = jnp.sum(a * b, axis=1, keepdims=True) * HEAT
    loss_ref[...] = jnp.sum(jnp.log(t1) + jnp.log(t2) - 2.0 * match, axis=0, keepdims=True) * (
        1.0 / (2.0 * n_pair)
    )
    da = HEAT * (mm3(s1, r1) - 2.0 * b)
    put(out2, mm3(s2, HEAT * b, 0, 0) + mm2(pair_a, da, 0, 0), 0)
    send_part(1, out2, in2, 0)
    db = HEAT * (mm3(s2, r0) - 2.0 * a)
    put(out2, mm3(s1, HEAT * a, 0, 0) + mm2(pair_b, db, 0, 0), n_dom)
    send_part(1, out2, in2, 1)
    wait_all(1, out2, in2)
    get(in2, rec)

    tall = -(-feat // 16) * 16
    chunk = half_s.shape[2]

    def pack_sum(w, g):
        last = g[0:tall, 256:384]
        last = last[0 : tall // 2] + pltpu.roll(last[tall // 2 :], 64, 1)
        spare = jnp.zeros((n_dev * chunk - 5 * tall // 2, 128), F32)
        flat = jnp.concatenate([g[0:tall, 0:128], g[0:tall, 128:256], last, spare], axis=0)
        pk[w] = flat.reshape(n_graph, n_dom, chunk, 128)

    def pair_copy(w):
        return remote(
            pk.at[w, other], pair_in.at[w], pair_ss.at[w], pair_rs.at[w], (other, my_d)
        )

    def scatter_copy(w, d, land):
        return remote(
            half_s.at[w, d], rs_in.at[w, land], rs_ss.at[w, d], rs_rs.at[w, land], (my_g, d)
        )

    def gather_copy(w, d, land):
        return remote(
            red.at[w], fin.at[w, my_g, land], ag_ss.at[w, d], ag_rs.at[w, land], (my_g, d)
        )

    def each_chip(do):
        def step(k, carry):
            do(lax.rem(my_d + k, n_dom))
            return carry

        lax.fori_loop(1, n_dom, step, 0)

    def sum_scatter(w):
        pair_copy(w).wait()
        half_s[w] = pk[w, pl.ds(my_g, 1)].reshape(n_dom, chunk, 128) + pair_in[w]
        each_chip(lambda d: scatter_copy(w, d, my_d).start())

    def sum_gather(w):
        each_chip(lambda d: scatter_copy(w, d, d).wait())
        rs_in[w, pl.ds(my_d, 1)] = half_s[w, pl.ds(my_d, 1)]
        total = jnp.sum(rs_in[w], axis=0) * (1.0 / math.sqrt(rows * n_dev))
        red[w] = total
        fin[w, pl.ds(my_g, 1), pl.ds(my_d, 1)] = total.reshape(1, 1, chunk, 128)
        each_chip(lambda d: gather_copy(w, d, my_d).start())

    def back_copy(w, side):
        return remote(
            fin.at[w, my_g], fin.at[w, side], back_ss.at[w], back_rs.at[w], (other, my_d)
        )

    def sum_back(w):
        each_chip(lambda d: gather_copy(w, d, d).wait())
        back_copy(w, my_g).start()

    def sum_end(w, ref):
        back_copy(w, my_g).wait_send()
        back_copy(w, other).wait_recv()
        flat = fin[w].reshape(n_dev * chunk, 128)
        ref[:, 0:128] = flat[0:feat]
        ref[:, 128:256] = flat[tall : tall + feat]
        last = flat[2 * tall : 2 * tall + tall // 2]
        last = jnp.concatenate([last, pltpu.roll(last, 64, 1)], axis=0)
        ref[:, 256:feat] = last[0:feat, 0 : feat - 256]

    unit = unit_s[...]
    grad_unit = mm2(unroute, rec[...])
    grad_latent = (
        grad_unit - unit * jnp.sum(grad_unit * unit, axis=1, keepdims=True)
    ) * inv_len
    shared = grad_latent * inv
    send_halo(2, mm3(mm2(adj_t[rows:, :], shared), w2_s[...], 1, 1))
    pack_sum(1, mm3(mix2[...], grad_latent, 0, 0))
    pair_copy(1).start()
    own = mm2(adj_t[0:rows, :], mm3(shared, w2_s[...], 1, 1))
    sum_scatter(1)
    grad_hidden = own + mm2(unbound, take_halo(2))
    hidden = hid[...]
    grad_inner = grad_hidden * (1.0 - hidden * hidden)
    pack_sum(0, mm3(mix1[...], grad_inner, 0, 0))
    pair_copy(0).start()
    shared = grad_inner * inv
    send_halo(3, mm3(mm2(adj_t[rows:, :], shared), w1_s[...], 1, 1))
    sum_gather(1)
    sum_scatter(0)
    own = mm2(adj_t[0:rows, :], mm3(shared, w1_s[...], 1, 1))
    sum_back(1)
    sum_gather(0)
    grad_x = own + mm2(unbound, take_halo(3))
    gemb_ref[...] = grad_x[:, 0:feat]
    sum_end(1, g2_ref)
    sum_back(0)
    sum_end(0, g1_ref)


def on_device(
    embeddings,
    first_weight,
    second_weight,
    bound_index,
    neighbors,
    degree,
    send_index,
    recv_count,
    pair_index,
):
    rows, feat = embeddings.shape[1:]
    rim = bound_index.shape[-1]
    n_graph = lax.axis_size("graph")
    n_dom = lax.axis_size("dom")
    n_dev = n_graph * n_dom
    cap = send_index.shape[-1]
    n_pair = pair_index.shape[-1]
    slots = n_dev * cap
    wide = -(-feat // 128) * 128
    pool = rows + 2 * rim

    part = cap // 2 if cap % 16 == 0 else cap
    tall = -(-feat // 16) * 16
    chunk = -(-(5 * tall // 2) // (8 * n_dev)) * 8
    sem = pltpu.SemaphoreType.DMA
    vmem = pltpu.VMEM
    sizes = (n_graph, n_dom, cap, feat, rows, rim, n_pair)
    grad_emb, g1, g2, loss = pl.pallas_call(
        functools.partial(kernel, sizes),
        out_shape=(
            jax.ShapeDtypeStruct((rows, feat), F32),
            jax.ShapeDtypeStruct((feat, feat), F32),
            jax.ShapeDtypeStruct((feat, feat), F32),
            jax.ShapeDtypeStruct((1, 1), F32),
        ),
        in_specs=[pl.BlockSpec(memory_space=pltpu.VMEM)] * 9,
        out_specs=[pl.BlockSpec(memory_space=pltpu.VMEM)] * 4,
        scratch_shapes=[
            vmem((rows, wide), F32),
            vmem((wide, wide), F32),
            vmem((wide, wide), F32),
            vmem((8, slots), jnp.int32),
            vmem((slots, 8), jnp.int32),
            vmem((rows, pool), BF16),
            vmem((pool, rows), BF16),
            vmem((rows, wide), F32),
            vmem((rows, wide), F32),
            vmem((rows, wide), F32),
            vmem((rows, wide), F32),
            vmem((n_dev, 2 * cap + part, 128), F32),
            vmem((n_dev, 2 * cap + part, 128), F32),
            vmem((n_dev, 2 * cap + part, 128), F32),
            vmem((n_dev, 2 * cap + part, 128), F32),
            vmem((slots, wide), F32),
            vmem((4, 2, rim, wide), F32),
            vmem((4, 2, rim, wide), F32),
            vmem((2, n_graph, n_dom, chunk, 128), F32),
            vmem((2, n_dom, chunk, 128), F32),
            vmem((2, n_dom, chunk, 128), F32),
            vmem((2, n_dom, chunk, 128), F32),
            vmem((2, chunk, 128), F32),
            vmem((2, n_graph, n_dom, chunk, 128), F32),
            sem((4, 2)),
            sem((4, 2)),
            sem((2, n_dev)),
            sem((2, n_dev)),
            sem((2,)),
            sem((2,)),
            sem((2, n_dom)),
            sem((2, n_dom)),
            sem((2, n_dom)),
            sem((2, n_dom)),
            sem((2,)),
            sem((2,)),
        ],
        compiler_params=pltpu.CompilerParams(
            collective_id=0, has_side_effects=True, vmem_limit_bytes=50 * 1024 * 1024
        ),
    )(
        embeddings[0],
        first_weight,
        second_weight,
        neighbors[0].T,
        degree,
        send_index.reshape(1, slots),
        bound_index.reshape(1, 2 * rim),
        recv_count.reshape(n_dev, 1),
        pair_index[0, 0],
    )
    return grad_emb[None], g1, g2, loss


def solution(mesh):
    in_specs = (
        P("graph", "dom", None),
        P(),
        P(),
        P("graph", "dom", None, None),
        P("graph", "dom", None),
        P("graph", "dom"),
        P("graph", "dom", None, None),
        P("graph", "dom", None),
        P("graph", "dom", None, None),
    )
    out_specs = (P("graph", "dom", None), P(), P(), P("graph", "dom"))
    return jax.shard_map(
        on_device, mesh=mesh, in_specs=in_specs, out_specs=out_specs, check_vma=False
    )
```
